32 devices in a mesh: groups: 2 (over y), seq: 4 (over z), mp: 4 (over x, core).
Axes of the slice: x: 2, y: 2, z: 4, core: 2. Of those that a mesh axis runs over, the one named last changes fastest.
Arguments:
- hidden: bfloat16 [1024, 8192], P(('groups', 'seq'), 'mp'), parts along dimension 0, may hold values from -6 to 6
- queries: bfloat16 [1024, 4096], P(('groups', 'seq'), 'mp'), parts along dimension 0, may hold values from -68 to 68
- w_kv: bfloat16 [8192, 1024], P('mp', 'seq'), may hold values from -0.0625 to 0.0625
- parents: int32 [8], P('groups'), parts along dimension 0, may hold values from -1 to 2, as said below
- lengths: int32 [8], P('groups'), parts along dimension 0, may hold values from 32 to 128, as said below
Outputs:
- context: bfloat16 [1024, 4096], P(('groups', 'seq'), 'mp'), parts along dimension 0
The draws below stay inside these ranges and needn't reach their ends.
There are 2 independent parts, one for each index of `groups`. The reference program is written for one: setup_inputs(seed, part) draws one part's arguments, and reference() takes and returns one part's arrays. A program takes and returns all parts, laid end to end along the dimension named above; an argument that names none is the same for every part. Nothing has to cross between parts.
Inputs may be any that keep to these rules, and one draw needn't show every extreme that they name: parents[0] is -1; for i >= 1, parents[i] is -1 (a new root) or an earlier segment, below i; the last segment's parent is segment 4 - 2. `lengths`: segment 0 fills its block.
All inputs are finite; a program needn't handle non-finite values.
Results may differ from the reference program's by a relative error of at most 0.011.
Values may be sent and summed in bfloat16 or wider, within the bound.
A program may use at most 64 MiB of HBM per device.

```python
import math
import jax
import jax.numpy as jnp
from jax import lax

D = 8192
HD = 128
KVH = 4
QH = 32
BLOCK = 128
SEGS = 4
TOKENS = 512
KVW = 1024


def draw_queries(key, part):
    key = jax.random.fold_in(key, 23)
    first_key = jax.random.fold_in(key, 0)
    values = jnp.clip(jax.random.normal(first_key, (TOKENS, QH * HD)), -6.0, 6.0)
    return values.astype(jnp.float32).astype(jnp.bfloat16)


def draw_parents(key, part):
    key = jax.random.fold_in(key, 11)
    seg_ids = jnp.arange(SEGS, dtype=jnp.int32)
    raw_bits = jax.random.randint(key, (SEGS,), 0, 1 << 30, dtype=jnp.int32)
    parent_ids = raw_bits % (seg_ids + 1) - 1
    parent_ids = jnp.where(seg_ids == SEGS - 1, SEGS - 2, parent_ids)
    return jnp.where(seg_ids == 0, -1, parent_ids).astype(jnp.int32)


def draw_lengths(key, part):
    key = jax.random.fold_in(key, 37)
    seg_ids = jnp.arange(SEGS, dtype=jnp.int32)
    drawn = jax.random.randint(key, (SEGS,), BLOCK // 4, BLOCK + 1, dtype=jnp.int32)
    drawn = jnp.where(seg_ids == 0, BLOCK, drawn)
    return jnp.where(seg_ids == SEGS - 1, BLOCK // 4, drawn).astype(jnp.int32)


def shard_levels(stream_key, extent, pieces, low, largest):
    def one(dim, shards_of):
        heights = jax.random.uniform(jax.random.fold_in(jax.random.fold_in(stream_key, 6), dim), (shards_of,), jnp.float32, low / len(pieces), largest / len(pieces))
        return jnp.repeat(jnp.exp(heights), extent[dim] // shards_of).reshape((-1,) + (1,) * (len(extent) - dim - 1))

    level = one(*pieces[0])
    for cut in pieces[1:]:
        level = level * one(*cut)
    return level


def centred(key, extent, scale, limit, cuts=(), kind=jnp.bfloat16):
    loudness = shard_levels(key, extent, cuts, -0.22, 0.18) if cuts else 1.0
    values = jax.random.normal(key, extent, jnp.float32) * scale * loudness
    return jnp.minimum(jnp.maximum(values, -limit), limit).astype(kind)


def setup_inputs(seed: int = 0, part: int = 0) -> dict:
    splits = jax.random.split(jax.random.key(seed), 6)
    own_keys = jax.random.split(jax.random.fold_in(splits[5], part), 6)
    hidden = centred(own_keys[0], (TOKENS, D), 1.0, 6.0, ((0, 4), (1, 4)))
    queries = draw_queries(jax.random.fold_in(jax.random.fold_in(splits[5], part), 71), part)
    w_kv = centred(splits[2], (D, KVW), D ** -0.5, 0.0625, ((0, 4), (1, 4)))
    parents = draw_parents(jax.random.fold_in(jax.random.fold_in(splits[5], part), 71), part)
    lengths = draw_lengths(jax.random.fold_in(jax.random.fold_in(splits[5], part), 71), part)
    return dict(hidden=hidden, queries=queries, w_kv=w_kv, parents=parents, lengths=lengths)


def reach_table(parents, seg_count):
    seg_ids = jnp.arange(seg_count, dtype=jnp.int32)
    reach = (parents[:, None] == seg_ids[None, :]).astype(jnp.float32)
    for level in range(seg_count.bit_length()):
        reach = jnp.minimum(reach + jnp.dot(reach, reach, precision=lax.Precision.HIGHEST), 1.0)
    return reach

def reference(hidden, queries, w_kv, parents, lengths):
    key_value = jnp.dot(hidden, w_kv, preferred_element_type=jnp.float32).astype(jnp.bfloat16)
    key_value = lax.optimization_barrier(key_value).astype(jnp.float32)
    split_kv = key_value.reshape(TOKENS, KVH, 2, HD)
    all_keys = split_kv[:, :, 0]
    all_values = split_kv[:, :, 1]
    reach = reach_table(parents, SEGS)
    positions = jnp.arange(TOKENS, dtype=jnp.int32)
    key_block = positions // BLOCK
    key_offset = positions % BLOCK
    key_live = key_offset < lengths[key_block]
    q_offset = jnp.arange(BLOCK, dtype=jnp.int32)
    group = QH // KVH
    score_scale = 1.0 / math.sqrt(HD)

    def one_segment(segment):
        block_q = lax.dynamic_slice_in_dim(queries, (segment * BLOCK).astype(jnp.int32), BLOCK, 0)
        block_q = block_q.astype(jnp.float32).reshape(BLOCK, KVH, group, HD)
        own_block = key_block == segment
        allowed = key_live & (own_block | (reach[segment][key_block] > 0.5))
        key_mask = allowed[None, :] & (jnp.logical_not(own_block)[None, :] | (key_offset[None, :] <= q_offset[:, None]))
        scores = jnp.einsum('qhgd,khd->hgqk', block_q, all_keys) * score_scale
        scores = jnp.where(key_mask, scores, -1e+30)
        top = scores.max(-1, keepdims=True)
        weights = jnp.where(key_mask, jnp.exp(scores - top), 0.0)
        total = weights.sum(-1)
        rounded = lax.optimization_barrier(weights.astype(jnp.bfloat16)).astype(jnp.float32)
        summed = jnp.einsum('hgqk,khd->hgqd', rounded, all_values) / total[..., None]
        summed = summed.transpose(2, 0, 1, 3).reshape(BLOCK, QH * HD)
        live_rows = q_offset < lengths[segment]
        return jnp.where(live_rows[:, None], summed, 0.0).astype(jnp.bfloat16)
    blocks = lax.map(one_segment, jnp.arange(SEGS, dtype=jnp.int32))
    return blocks.reshape(TOKENS, QH * HD)
```

```python
import math

import jax
import jax.numpy as jnp
from jax import lax
from jax.experimental import pallas as pl
from jax.experimental.pallas import tpu as pltpu
from jax.sharding import PartitionSpec as P

HD = 128
KVH = 4
QH = 32
CHUNKS = 4
MESH = pl.DeviceIdType.MESH


def reach_table(parents, seg_count):
    seg_ids = jnp.arange(seg_count, dtype=jnp.int32)
    reach = (parents[:, None] == seg_ids[None, :]).astype(jnp.float32)
    for level in range(seg_count.bit_length()):
        reach = jnp.minimum(reach + jnp.dot(reach, reach, precision=lax.Precision.HIGHEST), 1.0)
    return reach


def body(hidden, queries, w_kv, parents, lengths):
    block_rows = hidden.shape[0]
    mp_count = lax.axis_size("mp")
    seq_count = lax.axis_size("seq")
    kv_heads = KVH // mp_count
    group = QH // KVH
    kv_terms = jnp.dot(
        hidden, lax.all_gather(w_kv, "seq", axis=1, tiled=True), preferred_element_type=jnp.float32
    )
    kv_sums = lax.psum_scatter(kv_terms, "mp", scatter_dimension=1, tiled=True)
    key_value = kv_sums.astype(jnp.bfloat16)
    my_index = lax.axis_index("seq")
    reach_row = reach_table(parents, seq_count)[my_index]
    query_heads = queries.reshape(block_rows, kv_heads, group, HD)
    q_offset = jnp.arange(block_rows, dtype=jnp.int32)
    score_scale = 1.0 / math.sqrt(HD)

    def update(carry, kv_block, allowed, own_block, k_offset):
        run_max, run_total, run_acc = carry
        split_kv = kv_block.reshape(kv_block.shape[0], kv_heads, 2, HD)
        scores = (
            jnp.einsum(
                "qhgd,khd->hgqk", query_heads, split_kv[:, :, 0], preferred_element_type=jnp.float32
            )
            * score_scale
        )
        key_mask = allowed[None, :] & (
            jnp.logical_not(own_block)[None, :] | (k_offset[None, :] <= q_offset[:, None])
        )
        scores = jnp.where(key_mask, scores, -1e30)
        new_max = jnp.maximum(run_max, scores.max(-1))
        factor = jnp.exp(run_max - new_max)
        weights = jnp.where(key_mask, jnp.exp(scores - new_max[..., None]), 0.0)
        run_total = run_total * factor + weights.sum(-1)
        run_acc = run_acc * factor[..., None] + jnp.einsum(
            "hgqk,khd->hgqd",
            weights.astype(jnp.bfloat16),
            split_kv[:, :, 1],
            preferred_element_type=jnp.float32,
        )
        return (new_max, run_total, run_acc)

    start_state = (
        jnp.full((kv_heads, group, block_rows), -1e30, jnp.float32),
        jnp.zeros((kv_heads, group, block_rows), jnp.float32),
        jnp.zeros((kv_heads, group, block_rows, HD), jnp.float32),
    )
    piece = lax.all_gather(key_value, "seq", axis=0, tiled=True)
    piece_rows = piece.shape[0]
    span = min(piece_rows, block_rows)

    def visit(position, state):
        kv_block = lax.dynamic_slice_in_dim(piece, position * span, span, 0)
        k_pos = position * span + jnp.arange(span, dtype=jnp.int32)
        k_block = k_pos // block_rows
        k_offset = k_pos % block_rows
        own_block = k_block == my_index
        allowed = (k_offset < lengths[k_block]) & (own_block | (reach_row[k_block] > 0.5))
        return lax.cond(
            jnp.any(allowed),
            lambda inner: update(inner, kv_block, allowed, own_block, k_offset),
            lambda inner: inner,
            state,
        )

    run_max, run_total, run_acc = lax.fori_loop(0, piece_rows // span, visit, start_state)
    summed = run_acc / run_total[..., None]
    summed = summed.transpose(2, 0, 1, 3).reshape(block_rows, kv_heads * group * HD)
    live_rows = q_offset < lengths[my_index]
    return jnp.where(live_rows[:, None], summed, 0.0).astype(jnp.bfloat16)


def tree_kernel(
    hidden_hbm, queries_hbm, w_hbm, parents_ref, lengths_ref, out_ref,
    hid, w, q, acc, red, fin, kv, bias,
    local_sem, hid_send, hid_recv, red_send, red_recv, kv_send, kv_recv,
):
    seq_count, rows, width = hid.shape
    mp_count = seq_count
    quarter = rows // mp_count
    chunk = width // CHUNKS
    head_cols = w.shape[1]
    z = lax.axis_index("seq")
    m = lax.axis_index("mp")

    hid_copy = pltpu.make_async_copy(hidden_hbm, hid.at[z], local_sem.at[0])
    w_copy = pltpu.make_async_copy(w_hbm, w, local_sem.at[1])
    q_copy = pltpu.make_async_copy(queries_hbm, q, local_sem.at[2])
    hid_copy.start()
    w_copy.start()
    q_copy.start()

    barrier = pltpu.get_barrier_semaphore()
    for dz in range(seq_count):
        for dm in range(mp_count):
            if dz or dm:
                pl.semaphore_signal(
                    barrier,
                    inc=1,
                    device_id={"seq": lax.rem(z + dz, seq_count), "mp": lax.rem(m + dm, mp_count)},
                    device_id_type=MESH,
                )

    acc[...] = jnp.zeros_like(acc)
    for seg in range(seq_count):
        @pl.when(z < seg)
        def _():
            kv[seg] = jnp.zeros(kv.shape[1:], kv.dtype)

    parent = [parents_ref[seg] for seg in range(seq_count)]
    def step_up(cur):
        up = jnp.int32(-1)
        for seg in range(seq_count):
            up = jnp.where(cur == seg, parent[seg], up)
        return up
    seen = [jnp.int32(0)] * seq_count
    cur = z
    for _ in range(seq_count - 1):
        cur = step_up(cur)
        seen = [jnp.where(cur == seg, 1, seen[seg]) for seg in range(seq_count)]
    q_pos = lax.broadcasted_iota(jnp.int32, (rows, rows), 0)
    k_pos = lax.broadcasted_iota(jnp.int32, (rows, rows), 1)
    my_length = jnp.int32(0)
    for seg in range(seq_count):
        own = z == seg
        my_length = jnp.where(own, lengths_ref[seg], my_length)
        limit = jnp.where((seen[seg] > 0) | own, lengths_ref[seg], 0)
        last = jnp.where(own, 0, rows)
        visible = (k_pos < limit) & (k_pos <= q_pos + last)
        bias[:, seg * rows:(seg + 1) * rows] = jnp.where(visible, 0.0, -1e30)

    pl.semaphore_wait(barrier, seq_count * mp_count - 1)
    hid_copy.wait()

    def columns(c):
        return pl.ds(pl.multiple_of(c * chunk, chunk), chunk)

    def hop(way, seg, c):
        target = z + 1 if way == 0 else z - 1
        return pltpu.make_async_remote_copy(
            src_ref=hid.at[seg, :, columns(c)],
            dst_ref=hid.at[seg, :, columns(c)],
            send_sem=hid_send.at[way, seg, c],
            recv_sem=hid_recv.at[seg, c],
            device_id={"seq": target},
            device_id_type=MESH,
        )

    def add_chunk(seg, c):
        term = jnp.dot(
            hid[seg, :, columns(c)], w[columns(c), :], preferred_element_type=jnp.float32
        )
        acc[seg] += term

    def to_peer(seg, d):
        peer = lax.rem(m + d, mp_count)
        return pltpu.make_async_remote_copy(
            src_ref=acc.at[seg, pl.ds(pl.multiple_of(peer * quarter, quarter), quarter), :],
            dst_ref=red.at[seg, d - 1],
            send_sem=red_send.at[seg, d - 1],
            recv_sem=red_recv.at[seg, d - 1],
            device_id={"mp": peer},
            device_id_type=MESH,
        )

    my_rows = pl.ds(pl.multiple_of(m * quarter, quarter), quarter)

    def to_reader(seg, reader):
        return pltpu.make_async_remote_copy(
            src_ref=fin.at[seg],
            dst_ref=kv.at[seg, my_rows, :],
            send_sem=kv_send.at[seg, reader],
            recv_sem=kv_recv.at[seg, m],
            device_id={"seq": reader, "mp": z},
            device_id_type=MESH,
        )

    def send_terms(seg):
        for d in range(1, mp_count):
            to_peer(seg, d).start()

    def finish(seg):
        total = acc[seg, my_rows, :]
        for d in range(1, mp_count):
            to_peer(seg, d).wait_recv()
            total = total + red[seg, d - 1]
        fin[seg] = total.astype(fin.dtype)
        for reader in range(seq_count):
            here = (z == reader) & (m == z)

            @pl.when((seg <= reader) & jnp.logical_not(here))
            def _():
                to_reader(seg, reader).start()

            @pl.when((seg <= reader) & here)
            def _():
                kv[seg, my_rows, :] = fin[seg]

    def when_seg(seg, action):
        @pl.when((seg >= 0) & (seg < seq_count))
        def _():
            action(seg)

    for c in range(CHUNKS):
        @pl.when(z < seq_count - 1)
        def _():
            hop(0, z, c).start()

        @pl.when(z > 0)
        def _():
            hop(1, z, c).start()

    w_copy.wait()

    @pl.loop(0, CHUNKS)
    def _(c):
        add_chunk(z, c)

    send_terms(z)

    for d in range(1, seq_count):
        below, above = z - d, z + d

        @pl.loop(0, CHUNKS)
        def _(c):
            @pl.when(below >= 0)
            def _():
                hop(0, below, c).wait_recv()

                @pl.when(z < seq_count - 1)
                def _():
                    hop(0, below, c).start()

            @pl.when(above < seq_count)
            def _():
                hop(1, above, c).wait_recv()

                @pl.when(z > 0)
                def _():
                    hop(1, above, c).start()

            @pl.when(below >= 0)
            def _():
                add_chunk(below, c)

            @pl.when(above < seq_count)
            def _():
                add_chunk(above, c)

        when_seg(below, send_terms)
        when_seg(above, send_terms)
        if d == 1:
            finish(z)
        else:
            when_seg(z - d + 1, finish)
            when_seg(z + d - 1, finish)
    when_seg(z - seq_count + 1, finish)
    when_seg(z + seq_count - 1, finish)

    q_copy.wait()
    for seg in range(seq_count):
        for part in range(mp_count):
            @pl.when((seg <= z) & ((z != m) | (m != part)))
            def _():
                pltpu.make_async_copy(
                    fin.at[seg], kv.at[seg, part * quarter:(part + 1) * quarter, :], kv_recv.at[seg, part]
                ).wait()

    keys = seq_count * rows
    scale = math.log2(math.e) / math.sqrt(HD)
    all_kv = kv[...].reshape(keys, head_cols)
    k_all = all_kv[:, :HD]
    v_all = all_kv[:, HD:]
    live = lax.broadcasted_iota(jnp.int32, (rows, HD), 0) < my_length
    for head in range(q.shape[1] // HD):
        cols = slice(head * HD, (head + 1) * HD)
        scores = lax.dot_general(
            q[:, cols], k_all, (((1,), (1,)), ((), ())), preferred_element_type=jnp.float32
        ) + bias[...]
        top = scores.max(-1, keepdims=True)
        weights = jnp.exp2((scores - top) * scale)
        total = weights.sum(-1, keepdims=True)
        summed = jnp.dot(
            weights.astype(jnp.bfloat16), v_all, preferred_element_type=jnp.float32
        ) / total
        out_ref[:, cols] = jnp.where(live, summed, 0.0).astype(out_ref.dtype)

    for c in range(CHUNKS):
        for seg in range(seq_count):
            @pl.when((seg <= z) & (z < seq_count - 1))
            def _():
                hop(0, seg, c).wait_send()

            @pl.when((seg >= z) & (z > 0))
            def _():
                hop(1, seg, c).wait_send()
    for seg in range(seq_count):
        for d in range(1, mp_count):
            to_peer(seg, d).wait_send()
        for reader in range(seg, seq_count):
            @pl.when((z != reader) | (m != z))
            def _():
                to_reader(seg, reader).wait_send()


def tree_body(hidden, queries, w_kv, parents, lengths):
    rows, width = hidden.shape
    head_cols = w_kv.shape[1]
    count = lax.axis_size("seq")
    quarter = rows // count
    any_space = pl.BlockSpec(memory_space=pl.ANY)
    smem = pl.BlockSpec(memory_space=pltpu.SMEM)
    dma = pltpu.SemaphoreType.DMA
    return pl.pallas_call(
        tree_kernel,
        out_shape=jax.ShapeDtypeStruct(queries.shape, jnp.bfloat16),
        in_specs=[any_space, any_space, any_space, smem, smem],
        out_specs=pl.BlockSpec(memory_space=pltpu.VMEM),
        scratch_shapes=[
            pltpu.VMEM((count, rows, width), jnp.bfloat16),
            pltpu.VMEM(w_kv.shape, jnp.bfloat16),
            pltpu.VMEM(queries.shape, jnp.bfloat16),
            pltpu.VMEM((count, rows, head_cols), jnp.float32),
            pltpu.VMEM((count, count - 1, quarter, head_cols), jnp.float32),
            pltpu.VMEM((count, quarter, head_cols), jnp.bfloat16),
            pltpu.VMEM((count, rows, head_cols), jnp.bfloat16),
            pltpu.VMEM((rows, count * rows), jnp.float32),
            dma((3,)),
            dma((2, count, CHUNKS)),
            dma((count, CHUNKS)),
            dma((count, count - 1)),
            dma((count, count - 1)),
            dma((count, count)),
            dma((count, count)),
        ],
        compiler_params=pltpu.CompilerParams(
            collective_id=0, has_side_effects=True, vmem_limit_bytes=40 * 1024 * 1024
        ),
    )(hidden, queries, w_kv, parents, lengths)


def solution(mesh):
    seq_count, mp_count = mesh.shape["seq"], mesh.shape["mp"]
    by_heads = seq_count == KVH and mp_count == KVH
    return jax.shard_map(
        tree_body if by_heads else body,
        mesh=mesh,
        in_specs=(
            P(("groups", "seq"), "mp"),
            P(("groups", "seq"), "mp"),
            P("mp", "seq"),
            P("groups"),
            P("groups"),
        ),
        out_specs=P(("groups", "seq"), "mp"),
        check_vma=False,
    )
```

```python
import math

import jax
import jax.numpy as jnp
from jax import lax
from jax.experimental import pallas as pl
from jax.experimental.pallas import tpu as pltpu
from jax.sharding import PartitionSpec as P

HD = 128
KVH = 4
QH = 32
CHUNKS = 4
HALF = CHUNKS // 2
MESH = pl.DeviceIdType.MESH


def reach_table(parents, seg_count):
    seg_ids = jnp.arange(seg_count, dtype=jnp.int32)
    reach = (parents[:, None] == seg_ids[None, :]).astype(jnp.float32)
    for level in range(seg_count.bit_length()):
        reach = jnp.minimum(reach + jnp.dot(reach, reach, precision=lax.Precision.HIGHEST), 1.0)
    return reach


def body(hidden, queries, w_kv, parents, lengths):
    block_rows = hidden.shape[0]
    mp_count = lax.axis_size("mp")
    seq_count = lax.axis_size("seq")
    kv_heads = KVH // mp_count
    group = QH // KVH
    kv_terms = jnp.dot(
        hidden, lax.all_gather(w_kv, "seq", axis=1, tiled=True), preferred_element_type=jnp.float32
    )
    kv_sums = lax.psum_scatter(kv_terms, "mp", scatter_dimension=1, tiled=True)
    key_value = kv_sums.astype(jnp.bfloat16)
    my_index = lax.axis_index("seq")
    reach_row = reach_table(parents, seq_count)[my_index]
    query_heads = queries.reshape(block_rows, kv_heads, group, HD)
    q_offset = jnp.arange(block_rows, dtype=jnp.int32)
    score_scale = 1.0 / math.sqrt(HD)

    def update(carry, kv_block, allowed, own_block, k_offset):
        run_max, run_total, run_acc = carry
        split_kv = kv_block.reshape(kv_block.shape[0], kv_heads, 2, HD)
        scores = (
            jnp.einsum(
                "qhgd,khd->hgqk", query_heads, split_kv[:, :, 0], preferred_element_type=jnp.float32
            )
            * score_scale
        )
        key_mask = allowed[None, :] & (
            jnp.logical_not(own_block)[None, :] | (k_offset[None, :] <= q_offset[:, None])
        )
        scores = jnp.where(key_mask, scores, -1e30)
        new_max = jnp.maximum(run_max, scores.max(-1))
        factor = jnp.exp(run_max - new_max)
        weights = jnp.where(key_mask, jnp.exp(scores - new_max[..., None]), 0.0)
        run_total = run_total * factor + weights.sum(-1)
        run_acc = run_acc * factor[..., None] + jnp.einsum(
            "hgqk,khd->hgqd",
            weights.astype(jnp.bfloat16),
            split_kv[:, :, 1],
            preferred_element_type=jnp.float32,
        )
        return (new_max, run_total, run_acc)

    start_state = (
        jnp.full((kv_heads, group, block_rows), -1e30, jnp.float32),
        jnp.zeros((kv_heads, group, block_rows), jnp.float32),
        jnp.zeros((kv_heads, group, block_rows, HD), jnp.float32),
    )
    piece = lax.all_gather(key_value, "seq", axis=0, tiled=True)
    piece_rows = piece.shape[0]
    span = min(piece_rows, block_rows)

    def visit(position, state):
        kv_block = lax.dynamic_slice_in_dim(piece, position * span, span, 0)
        k_pos = position * span + jnp.arange(span, dtype=jnp.int32)
        k_block = k_pos // block_rows
        k_offset = k_pos % block_rows
        own_block = k_block == my_index
        allowed = (k_offset < lengths[k_block]) & (own_block | (reach_row[k_block] > 0.5))
        return lax.cond(
            jnp.any(allowed),
            lambda inner: update(inner, kv_block, allowed, own_block, k_offset),
            lambda inner: inner,
            state,
        )

    run_max, run_total, run_acc = lax.fori_loop(0, piece_rows // span, visit, start_state)
    summed = run_acc / run_total[..., None]
    summed = summed.transpose(2, 0, 1, 3).reshape(block_rows, kv_heads * group * HD)
    live_rows = q_offset < lengths[my_index]
    return jnp.where(live_rows[:, None], summed, 0.0).astype(jnp.bfloat16)


def tree_kernel(
    hidden_hbm, queries_hbm, w_hbm, parents_hbm, lengths_hbm, out_ref,
    hid, w, w_outer, q, acc, acc_outer, red, fin, kv, bias, parents_ref, lengths_ref,
    local_sem, hid_send, hid_recv, w_send, w_recv, red_send, red_recv,
    outer_send, kv_send, kv_recv,
):
    seq_count, rows, width = hid.shape
    mp_count = seq_count
    quarter = rows // mp_count
    chunk = width // CHUNKS
    head_cols = w.shape[1]
    z = lax.axis_index("seq")
    m = lax.axis_index("mp")
    is_end = (z == 0) | (z == seq_count - 1)
    inner = jnp.where(z == 0, 1, seq_count - 2)
    inward = jnp.where(z < seq_count // 2, 1, -1)

    hid_copy = pltpu.make_async_copy(hidden_hbm, hid.at[z], local_sem.at[0])
    w_copy = pltpu.make_async_copy(w_hbm, w, local_sem.at[1])
    q_copy = pltpu.make_async_copy(queries_hbm, q, local_sem.at[2])
    parents_copy = pltpu.make_async_copy(parents_hbm, parents_ref, local_sem.at[3])
    lengths_copy = pltpu.make_async_copy(lengths_hbm, lengths_ref, local_sem.at[4])
    hid_copy.start()
    parents_copy.start()
    lengths_copy.start()
    w_copy.start()
    q_copy.start()

    barrier = pltpu.get_barrier_semaphore()
    for dz in range(seq_count):
        for dm in range(mp_count):
            if dz or dm:
                pl.semaphore_signal(
                    barrier,
                    inc=1,
                    device_id={"seq": lax.rem(z + dz, seq_count), "mp": lax.rem(m + dm, mp_count)},
                    device_id_type=MESH,
                )

    acc[...] = jnp.zeros_like(acc)
    for seg in range(seq_count):
        @pl.when(z < seg)
        def _():
            kv[seg] = jnp.zeros(kv.shape[1:], kv.dtype)

    parents_copy.wait()
    lengths_copy.wait()
    parent = [parents_ref[seg] for seg in range(seq_count)]
    def step_up(cur):
        up = jnp.int32(-1)
        for seg in range(seq_count):
            up = jnp.where(cur == seg, parent[seg], up)
        return up
    seen = [jnp.int32(0)] * seq_count
    cur = z
    for _ in range(seq_count - 1):
        cur = step_up(cur)
        seen = [jnp.where(cur == seg, 1, seen[seg]) for seg in range(seq_count)]
    q_pos = lax.broadcasted_iota(jnp.int32, (rows, rows), 0)
    k_pos = lax.broadcasted_iota(jnp.int32, (rows, rows), 1)
    my_length = jnp.int32(0)
    for seg in range(seq_count):
        own = z == seg
        my_length = jnp.where(own, lengths_ref[seg], my_length)
        limit = jnp.where((seen[seg] > 0) | own, lengths_ref[seg], 0)
        last = jnp.where(own, 0, rows)
        visible = (k_pos < limit) & (k_pos <= q_pos + last)
        bias[:, seg * rows:(seg + 1) * rows] = jnp.where(visible, 0.0, -1e30)

    pl.semaphore_wait(barrier, seq_count * mp_count - 1)
    hid_copy.wait()

    def columns(c):
        return pl.ds(pl.multiple_of(c * chunk, chunk), chunk)

    def hop(way, seg, c):
        target = z + 1 if way == 0 else z - 1
        return pltpu.make_async_remote_copy(
            src_ref=hid.at[seg, :, columns(c)],
            dst_ref=hid.at[seg, :, columns(c)],
            send_sem=hid_send.at[way, seg, c],
            recv_sem=hid_recv.at[seg, c],
            device_id={"seq": target},
            device_id_type=MESH,
        )

    def add_chunk(seg, c):
        term = jnp.dot(
            hid[seg, :, columns(c)], w[columns(c), :], preferred_element_type=jnp.float32
        )
        acc[seg] += term

    def w_hop(c):
        return pltpu.make_async_remote_copy(
            src_ref=w.at[columns(c), :],
            dst_ref=w_outer.at[columns(c - HALF), :],
            send_sem=w_send.at[c - HALF],
            recv_sem=w_recv.at[c - HALF],
            device_id={"seq": inner},
            device_id_type=MESH,
        )

    def to_outer(step, d):
        peer = lax.rem(m + d, mp_count)
        return pltpu.make_async_remote_copy(
            src_ref=acc_outer.at[step, pl.ds(pl.multiple_of(peer * quarter, quarter), quarter), :],
            dst_ref=red.at[z + step * inward, mp_count - 1 + d],
            send_sem=outer_send.at[step, d],
            recv_sem=red_recv.at[z + step * inward, mp_count - 1 + d],
            device_id={"seq": z - inward, "mp": peer},
            device_id_type=MESH,
        )

    def help_outer(step):
        seg = z + step * inward
        acc_outer[step] = jnp.dot(
            hid[seg, :, HALF * chunk:], w_outer[...], preferred_element_type=jnp.float32
        )
        for d in range(mp_count):
            to_outer(step, d).start()

    def to_peer(seg, d):
        peer = lax.rem(m + d, mp_count)
        return pltpu.make_async_remote_copy(
            src_ref=acc.at[seg, pl.ds(pl.multiple_of(peer * quarter, quarter), quarter), :],
            dst_ref=red.at[seg, d - 1],
            send_sem=red_send.at[seg, d - 1],
            recv_sem=red_recv.at[seg, d - 1],
            device_id={"mp": peer},
            device_id_type=MESH,
        )

    my_rows = pl.ds(pl.multiple_of(m * quarter, quarter), quarter)

    def to_reader(seg, reader):
        return pltpu.make_async_remote_copy(
            src_ref=fin.at[seg],
            dst_ref=kv.at[seg, my_rows, :],
            send_sem=kv_send.at[seg, reader],
            recv_sem=kv_recv.at[seg, m],
            device_id={"seq": reader, "mp": z},
            device_id_type=MESH,
        )

    def send_terms(seg):
        for d in range(1, mp_count):
            to_peer(seg, d).start()

    def finish(seg):
        total = acc[seg, my_rows, :]
        for d in range(1, mp_count):
            to_peer(seg, d).wait_recv()
            total = total + red[seg, d - 1]
        acc[seg, my_rows, :] = total

        @pl.when(is_end & (seg != z))
        def _():
            rest = acc[seg, my_rows, :]
            for d in range(mp_count):
                slot = mp_count - 1 + d
                pltpu.make_async_copy(
                    red.at[seg, slot], red.at[seg, slot], red_recv.at[seg, slot]
                ).wait()
                rest = rest + red[seg, slot]
            acc[seg, my_rows, :] = rest

        fin[seg] = acc[seg, my_rows, :].astype(fin.dtype)
        for reader in range(seq_count):
            here = (z == reader) & (m == z)

            @pl.when((seg <= reader) & jnp.logical_not(here))
            def _():
                to_reader(seg, reader).start()

            @pl.when((seg <= reader) & here)
            def _():
                kv[seg, my_rows, :] = fin[seg]

    def when_seg(seg, action):
        @pl.when((seg >= 0) & (seg < seq_count))
        def _():
            action(seg)

    def goes_up(c):
        return (z < seq_count - 1) if c < HALF else (z < seq_count - 2)

    def goes_down(c):
        return (z > 0) if c < HALF else (z > 1)

    def send_own(c):
        @pl.when(goes_up(c))
        def _():
            hop(0, z, c).start()

        @pl.when(goes_down(c))
        def _():
            hop(1, z, c).start()

    for c in range(HALF):
        send_own(c)
    w_copy.wait()

    @pl.when(is_end)
    def _():
        for c in range(HALF, CHUNKS):
            w_hop(c).start()

    for c in range(HALF, CHUNKS):
        send_own(c)

    @pl.loop(0, CHUNKS)
    def _(c):
        add_chunk(z, c)

    send_terms(z)

    def pass_on(below, above, first):
        has_below = (below >= 0) if first < HALF else (below >= 0) & jnp.logical_not(is_end)
        has_above = (above < seq_count) if first < HALF else (above < seq_count) & jnp.logical_not(is_end)

        @pl.loop(first, first + HALF)
        def _(c):
            @pl.when(has_below)
            def _():
                hop(0, below, c).wait_recv()

                @pl.when(goes_up(first))
                def _():
                    hop(0, below, c).start()

            @pl.when(has_above)
            def _():
                hop(1, above, c).wait_recv()

                @pl.when(goes_down(first))
                def _():
                    hop(1, above, c).start()

            @pl.when(has_below)
            def _():
                add_chunk(below, c)

            @pl.when(has_above)
            def _():
                add_chunk(above, c)

    is_inner = jnp.logical_not(is_end)
    for d in range(1, seq_count):
        below, above = z - d, z + d
        pass_on(below, above, 0)
        if d == 2:
            @pl.when(is_inner)
            def _():
                for c in range(HALF, CHUNKS):
                    w_hop(c).wait_recv()
                help_outer(0)
                help_outer(1)

        if d < seq_count - 1:
            pass_on(below, above, HALF)
        if d == 2:
            @pl.when(is_inner)
            def _():
                help_outer(2)

        when_seg(below, send_terms)
        when_seg(above, send_terms)
        if d == 1:
            finish(z)
        else:
            when_seg(z - d + 1, finish)
            when_seg(z + d - 1, finish)
    when_seg(z - seq_count + 1, finish)
    when_seg(z + seq_count - 1, finish)

    q_copy.wait()
    for seg in range(seq_count):
        for part in range(mp_count):
            @pl.when((seg <= z) & ((z != m) | (m != part)))
            def _():
                pltpu.make_async_copy(
                    fin.at[seg], kv.at[seg, part * quarter:(part + 1) * quarter, :], kv_recv.at[seg, part]
                ).wait()

    keys = seq_count * rows
    scale = math.log2(math.e) / math.sqrt(HD)
    all_kv = kv[...].reshape(keys, head_cols)
    k_all = all_kv[:, :HD]
    v_all = all_kv[:, HD:]
    live = lax.broadcasted_iota(jnp.int32, (rows, HD), 0) < my_length
    for head in range(q.shape[1] // HD):
        cols = slice(head * HD, (head + 1) * HD)
        scores = lax.dot_general(
            q[:, cols], k_all, (((1,), (1,)), ((), ())), preferred_element_type=jnp.float32
        ) + bias[...]
        top = scores.max(-1, keepdims=True)
        weights = jnp.exp2((scores - top) * scale)
        total = weights.sum(-1, keepdims=True)
        summed = jnp.dot(
            weights.astype(jnp.bfloat16), v_all, preferred_element_type=jnp.float32
        ) / total
        out_ref[:, cols] = jnp.where(live, summed, 0.0).astype(out_ref.dtype)

    for c in range(CHUNKS):
        for seg in range(seq_count):
            @pl.when((seg <= z) & goes_up(c))
            def _():
                hop(0, seg, c).wait_send()

            @pl.when((seg >= z) & goes_down(c))
            def _():
                hop(1, seg, c).wait_send()

    @pl.when(is_end)
    def _():
        for c in range(HALF, CHUNKS):
            w_hop(c).wait_send()

    @pl.when(is_inner)
    def _():
        for step in range(seq_count - 1):
            for d in range(mp_count):
                to_outer(step, d).wait_send()

    for seg in range(seq_count):
        for d in range(1, mp_count):
            to_peer(seg, d).wait_send()
        for reader in range(seg, seq_count):
            @pl.when((z != reader) | (m != z))
            def _():
                to_reader(seg, reader).wait_send()


def tree_body(hidden, queries, w_kv, parents, lengths):
    rows, width = hidden.shape
    head_cols = w_kv.shape[1]
    count = lax.axis_size("seq")
    quarter = rows // count
    any_space = pl.BlockSpec(memory_space=pl.ANY)
    dma = pltpu.SemaphoreType.DMA
    return pl.pallas_call(
        tree_kernel,
        out_shape=jax.ShapeDtypeStruct(queries.shape, jnp.bfloat16),
        in_specs=[any_space] * 5,
        out_specs=pl.BlockSpec(memory_space=pltpu.VMEM),
        scratch_shapes=[
            pltpu.VMEM((count, rows, width), jnp.bfloat16),
            pltpu.VMEM(w_kv.shape, jnp.bfloat16),
            pltpu.VMEM((w_kv.shape[0] // 2, head_cols), jnp.bfloat16),
            pltpu.VMEM(queries.shape, jnp.bfloat16),
            pltpu.VMEM((count, rows, head_cols), jnp.float32),
            pltpu.VMEM((count - 1, rows, head_cols), jnp.float32),
            pltpu.VMEM((count, 2 * count - 1, quarter, head_cols), jnp.float32),
            pltpu.VMEM((count, quarter, head_cols), jnp.bfloat16),
            pltpu.VMEM((count, rows, head_cols), jnp.bfloat16),
            pltpu.VMEM((rows, count * rows), jnp.float32),
            pltpu.SMEM(parents.shape, jnp.int32),
            pltpu.SMEM(lengths.shape, jnp.int32),
            dma((5,)),
            dma((2, count, CHUNKS)),
            dma((count, CHUNKS)),
            dma((HALF,)),
            dma((HALF,)),
            dma((count, count - 1)),
            dma((count, 2 * count - 1)),
            dma((count - 1, count)),
            dma((count, count)),
            dma((count, count)),
        ],
        compiler_params=pltpu.CompilerParams(
            collective_id=0, has_side_effects=True, vmem_limit_bytes=56 * 1024 * 1024
        ),
    )(hidden, queries, w_kv, parents, lengths)


def solution(mesh):
    seq_count, mp_count = mesh.shape["seq"], mesh.shape["mp"]
    by_heads = seq_count == KVH and mp_count == KVH
    return jax.shard_map(
        tree_body if by_heads else body,
        mesh=mesh,
        in_specs=(
            P(("groups", "seq"), "mp"),
            P(("groups", "seq"), "mp"),
            P("mp", "seq"),
            P("groups"),
            P("groups"),
        ),
        out_specs=P(("groups", "seq"), "mp"),
        check_vma=False,
    )
```

```python
import math

import jax
import jax.numpy as jnp
from jax import lax
from jax.experimental import pallas as pl
from jax.experimental.pallas import tpu as pltpu
from jax.sharding import PartitionSpec as P

HD = 128
KVH = 4
QH = 32
CHUNKS = 4
HALF = CHUNKS // 2
MESH = pl.DeviceIdType.MESH


def reach_table(parents, seg_count):
    seg_ids = jnp.arange(seg_count, dtype=jnp.int32)
    reach = (parents[:, None] == seg_ids[None, :]).astype(jnp.float32)
    for level in range(seg_count.bit_length()):
        reach = jnp.minimum(reach + jnp.dot(reach, reach, precision=lax.Precision.HIGHEST), 1.0)
    return reach


def body(hidden, queries, w_kv, parents, lengths):
    block_rows = hidden.shape[0]
    mp_count = lax.axis_size("mp")
    seq_count = lax.axis_size("seq")
    kv_heads = KVH // mp_count
    group = QH // KVH
    kv_terms = jnp.dot(
        hidden, lax.all_gather(w_kv, "seq", axis=1, tiled=True), preferred_element_type=jnp.float32
    )
    kv_sums = lax.psum_scatter(kv_terms, "mp", scatter_dimension=1, tiled=True)
    key_value = kv_sums.astype(jnp.bfloat16)
    my_index = lax.axis_index("seq")
    reach_row = reach_table(parents, seq_count)[my_index]
    query_heads = queries.reshape(block_rows, kv_heads, group, HD)
    q_offset = jnp.arange(block_rows, dtype=jnp.int32)
    score_scale = 1.0 / math.sqrt(HD)

    def update(carry, kv_block, allowed, own_block, k_offset):
        run_max, run_total, run_acc = carry
        split_kv = kv_block.reshape(kv_block.shape[0], kv_heads, 2, HD)
        scores = (
            jnp.einsum(
                "qhgd,khd->hgqk", query_heads, split_kv[:, :, 0], preferred_element_type=jnp.float32
            )
            * score_scale
        )
        key_mask = allowed[None, :] & (
            jnp.logical_not(own_block)[None, :] | (k_offset[None, :] <= q_offset[:, None])
        )
        scores = jnp.where(key_mask, scores, -1e30)
        new_max = jnp.maximum(run_max, scores.max(-1))
        factor = jnp.exp(run_max - new_max)
        weights = jnp.where(key_mask, jnp.exp(scores - new_max[..., None]), 0.0)
        run_total = run_total * factor + weights.sum(-1)
        run_acc = run_acc * factor[..., None] + jnp.einsum(
            "hgqk,khd->hgqd",
            weights.astype(jnp.bfloat16),
            split_kv[:, :, 1],
            preferred_element_type=jnp.float32,
        )
        return (new_max, run_total, run_acc)

    start_state = (
        jnp.full((kv_heads, group, block_rows), -1e30, jnp.float32),
        jnp.zeros((kv_heads, group, block_rows), jnp.float32),
        jnp.zeros((kv_heads, group, block_rows, HD), jnp.float32),
    )
    piece = lax.all_gather(key_value, "seq", axis=0, tiled=True)
    piece_rows = piece.shape[0]
    span = min(piece_rows, block_rows)

    def visit(position, state):
        kv_block = lax.dynamic_slice_in_dim(piece, position * span, span, 0)
        k_pos = position * span + jnp.arange(span, dtype=jnp.int32)
        k_block = k_pos // block_rows
        k_offset = k_pos % block_rows
        own_block = k_block == my_index
        allowed = (k_offset < lengths[k_block]) & (own_block | (reach_row[k_block] > 0.5))
        return lax.cond(
            jnp.any(allowed),
            lambda inner: update(inner, kv_block, allowed, own_block, k_offset),
            lambda inner: inner,
            state,
        )

    run_max, run_total, run_acc = lax.fori_loop(0, piece_rows // span, visit, start_state)
    summed = run_acc / run_total[..., None]
    summed = summed.transpose(2, 0, 1, 3).reshape(block_rows, kv_heads * group * HD)
    live_rows = q_offset < lengths[my_index]
    return jnp.where(live_rows[:, None], summed, 0.0).astype(jnp.bfloat16)


def tree_kernel(
    hidden_hbm, queries_hbm, w_hbm, parents_hbm, lengths_hbm, out_ref,
    hid, w, w_outer, q, acc, red, fin, kv, bias, parents_ref, lengths_ref,
    local_sem, hid_send, hid_recv, w_send, w_recv, red_send, red_recv, kv_send, kv_recv,
):
    seq_count, rows, width = hid.shape
    mp_count = seq_count
    quarter = rows // mp_count
    chunk = width // CHUNKS
    head_cols = w.shape[1]
    z = lax.axis_index("seq")
    m = lax.axis_index("mp")
    g = lax.axis_index("groups")
    is_end = (z == 0) | (z == seq_count - 1)
    is_inner = jnp.logical_not(is_end)
    inner = jnp.where(z == 0, 1, seq_count - 2)
    outer = jnp.where(z < seq_count // 2, 0, seq_count - 1)
    farthest = seq_count - 1 - outer
    extra = seq_count
    depth = w.shape[0] // 2
    piece = depth // CHUNKS

    hid_copy = pltpu.make_async_copy(hidden_hbm, hid.at[z], local_sem.at[0])
    w_copy = pltpu.make_async_copy(w_hbm, w, local_sem.at[1])
    q_copy = pltpu.make_async_copy(queries_hbm, q, local_sem.at[2])
    parents_copy = pltpu.make_async_copy(parents_hbm, parents_ref, local_sem.at[3])
    lengths_copy = pltpu.make_async_copy(lengths_hbm, lengths_ref, local_sem.at[4])
    hid_copy.start()
    parents_copy.start()
    lengths_copy.start()
    w_copy.start()
    q_copy.start()

    barrier = pltpu.get_barrier_semaphore()
    for dz in range(seq_count):
        for dm in range(mp_count):
            if dz or dm:
                pl.semaphore_signal(
                    barrier,
                    inc=1,
                    device_id={"seq": lax.rem(z + dz, seq_count), "mp": lax.rem(m + dm, mp_count)},
                    device_id_type=MESH,
                )

    pl.semaphore_signal(barrier, inc=1, device_id={"groups": 1 - g}, device_id_type=MESH)

    acc[...] = jnp.zeros_like(acc)
    for seg in range(seq_count):
        @pl.when(z < seg)
        def _():
            kv[seg] = jnp.zeros(kv.shape[1:], kv.dtype)

    parents_copy.wait()
    lengths_copy.wait()
    parent = [parents_ref[seg] for seg in range(seq_count)]
    def step_up(cur):
        up = jnp.int32(-1)
        for seg in range(seq_count):
            up = jnp.where(cur == seg, parent[seg], up)
        return up
    seen = [jnp.int32(0)] * seq_count
    cur = z
    for _ in range(seq_count - 1):
        cur = step_up(cur)
        seen = [jnp.where(cur == seg, 1, seen[seg]) for seg in range(seq_count)]
    q_pos = lax.broadcasted_iota(jnp.int32, (rows, rows), 0)
    k_pos = lax.broadcasted_iota(jnp.int32, (rows, rows), 1)
    my_length = jnp.int32(0)
    for seg in range(seq_count):
        own = z == seg
        my_length = jnp.where(own, lengths_ref[seg], my_length)
        limit = jnp.where((seen[seg] > 0) | own, lengths_ref[seg], 0)
        last = jnp.where(own, 0, rows)
        visible = (k_pos < limit) & (k_pos <= q_pos + last)
        bias[:, seg * rows:(seg + 1) * rows] = jnp.where(visible, 0.0, -1e30)

    pl.semaphore_wait(barrier, seq_count * mp_count)
    hid_copy.wait()

    def columns(c):
        return pl.ds(pl.multiple_of(c * chunk, chunk), chunk)

    def hop(way, seg, c):
        target = z + 1 if way == 0 else z - 1
        return pltpu.make_async_remote_copy(
            src_ref=hid.at[seg, :, columns(c)],
            dst_ref=hid.at[seg, :, columns(c)],
            send_sem=hid_send.at[way, seg, c],
            recv_sem=hid_recv.at[seg, c],
            device_id={"seq": target},
            device_id_type=MESH,
        )

    def add_chunk(seg, c):
        term = jnp.dot(
            hid[seg, :, columns(c)], w[columns(c), :], preferred_element_type=jnp.float32
        )
        acc[seg] += term

    def w_rows(half, c):
        return pl.ds(pl.multiple_of(half * depth + c * piece, piece), piece)

    def w_hop(c):
        return pltpu.make_async_remote_copy(
            src_ref=w.at[w_rows(g, c), :],
            dst_ref=w_outer.at[w_rows(g, c), :],
            send_sem=w_send.at[0, c],
            recv_sem=w_recv.at[0, c],
            device_id={"seq": inner},
            device_id_type=MESH,
        )

    def w_share(c):
        return pltpu.make_async_remote_copy(
            src_ref=w_outer.at[w_rows(g, c), :],
            dst_ref=w_outer.at[w_rows(g, c), :],
            send_sem=w_send.at[1, c],
            recv_sem=w_recv.at[1, c],
            device_id={"groups": 1 - g},
            device_id_type=MESH,
        )

    def add_half(half):
        part = pl.ds(pl.multiple_of(half * depth, depth), depth)
        acc[extra] += jnp.dot(
            hid[farthest, :, part], w_outer[part, :], preferred_element_type=jnp.float32
        )

    def to_peer(seg, d):
        peer = lax.rem(m + d, mp_count)
        return pltpu.make_async_remote_copy(
            src_ref=acc.at[seg, pl.ds(pl.multiple_of(peer * quarter, quarter), quarter), :],
            dst_ref=red.at[seg, d - 1],
            send_sem=red_send.at[seg, d - 1],
            recv_sem=red_recv.at[seg, d - 1],
            device_id={"mp": peer},
            device_id_type=MESH,
        )

    my_rows = pl.ds(pl.multiple_of(m * quarter, quarter), quarter)

    def to_reader(slot, reader):
        seg = jnp.where(slot == extra, farthest, slot)
        head = jnp.where(slot == extra, outer, z)
        return pltpu.make_async_remote_copy(
            src_ref=fin.at[slot],
            dst_ref=kv.at[seg, my_rows, :],
            send_sem=kv_send.at[slot, reader],
            recv_sem=kv_recv.at[seg, m],
            device_id={"seq": reader, "mp": head},
            device_id_type=MESH,
        )

    def send_terms(seg):
        for d in range(1, mp_count):
            to_peer(seg, d).start()

    def is_sent(slot, reader):
        seg = jnp.where(slot == extra, farthest, slot)
        head = jnp.where(slot == extra, outer, z)
        here = (z == reader) & (m == head)
        return (seg <= reader) & jnp.logical_not(here), (seg <= reader) & here

    def finish(slot):
        total = acc[slot, my_rows, :]
        for d in range(1, mp_count):
            to_peer(slot, d).wait_recv()
            total = total + red[slot, d - 1]
        fin[slot] = total.astype(fin.dtype)
        for reader in range(seq_count):
            away, here = is_sent(slot, reader)

            @pl.when(away)
            def _():
                to_reader(slot, reader).start()

            @pl.when(here)
            def _():
                kv[jnp.where(slot == extra, farthest, slot), my_rows, :] = fin[slot]

    def when_seg(seg, action):
        @pl.when((seg >= 0) & (seg < seq_count))
        def _():
            action(seg)

    for c in range(CHUNKS):
        @pl.when(z < seq_count - 1)
        def _():
            hop(0, z, c).start()

        @pl.when(z > 0)
        def _():
            hop(1, z, c).start()

    w_copy.wait()

    @pl.loop(0, CHUNKS)
    def _(c):
        add_chunk(z, c)

    send_terms(z)

    def pass_on(d, first):
        below, above = z - d, z + d
        forward = d < seq_count - 2

        @pl.loop(first, first + HALF)
        def _(c):
            @pl.when(below >= 0)
            def _():
                hop(0, below, c).wait_recv()
                if forward:
                    @pl.when(z < seq_count - 1)
                    def _():
                        hop(0, below, c).start()

            @pl.when(above < seq_count)
            def _():
                hop(1, above, c).wait_recv()
                if forward:
                    @pl.when(z > 0)
                    def _():
                        hop(1, above, c).start()

            @pl.when(below >= 0)
            def _():
                add_chunk(below, c)

            @pl.when(above < seq_count)
            def _():
                add_chunk(above, c)

    def share_w(first):
        @pl.when(is_inner)
        def _():
            for c in range(first, first + HALF):
                w_hop(c).wait_recv()
                w_share(c).start()

    for d in range(1, seq_count - 1):
        pass_on(d, 0)
        if d == seq_count - 2:
            share_w(0)
        if d == 1:
            finish(z)
        else:
            when_seg(z - d + 1, finish)
            when_seg(z + d - 1, finish)
        pass_on(d, HALF)
        if d == 1:
            @pl.when(is_end)
            def _():
                for c in range(CHUNKS):
                    @pl.when(z == 0)
                    def _():
                        hop(0, z, c).wait_send()

                    @pl.when(z > 0)
                    def _():
                        hop(1, z, c).wait_send()

                for c in range(CHUNKS):
                    w_hop(c).start()

        if d == seq_count - 2:
            share_w(HALF)
        when_seg(z - d, send_terms)
        when_seg(z + d, send_terms)

    @pl.when(is_inner)
    def _():
        add_half(g)
        for c in range(CHUNKS):
            w_share(c).wait_recv()
        add_half(1 - g)
        send_terms(extra)

    when_seg(z - seq_count + 2, finish)
    when_seg(z + seq_count - 2, finish)

    @pl.when(is_inner)
    def _():
        finish(jnp.int32(extra))

    q_copy.wait()
    for seg in range(seq_count):
        for part in range(mp_count):
            source = jnp.where((m == 0) & (seg == seq_count - 1), 1, m)
            source = jnp.where((m == seq_count - 1) & (seg == 0), seq_count - 2, source)

            @pl.when((seg <= z) & ((z != source) | (m != part)))
            def _():
                pltpu.make_async_copy(
                    fin.at[seg], kv.at[seg, part * quarter:(part + 1) * quarter, :], kv_recv.at[seg, part]
                ).wait()

    keys = seq_count * rows
    scale = math.log2(math.e) / math.sqrt(HD)
    all_kv = kv[...].reshape(keys, head_cols)
    k_all = all_kv[:, :HD]
    v_all = all_kv[:, HD:]
    live = lax.broadcasted_iota(jnp.int32, (rows, HD), 0) < my_length
    for head in range(q.shape[1] // HD):
        cols = slice(head * HD, (head + 1) * HD)
        scores = lax.dot_general(
            q[:, cols], k_all, (((1,), (1,)), ((), ())), preferred_element_type=jnp.float32
        ) + bias[...]
        top = scores.max(-1, keepdims=True)
        weights = jnp.exp2((scores - top) * scale)
        total = weights.sum(-1, keepdims=True)
        summed = jnp.dot(
            weights.astype(jnp.bfloat16), v_all, preferred_element_type=jnp.float32
        ) / total
        out_ref[:, cols] = jnp.where(live, summed, 0.0).astype(out_ref.dtype)

    for c in range(CHUNKS):
        for seg in range(seq_count):
            @pl.when((seg <= z) & (z - seg < seq_count - 2) & (z < seq_count - 1) & (z > 0))
            def _():
                hop(0, seg, c).wait_send()

            @pl.when((seg >= z) & (seg - z < seq_count - 2) & (z < seq_count - 1) & (z > 0))
            def _():
                hop(1, seg, c).wait_send()

        @pl.when(is_end)
        def _():
            w_hop(c).wait_send()

        @pl.when(is_inner)
        def _():
            w_share(c).wait_send()

    for slot in range(seq_count + 1):
        used = is_inner if slot == extra else (z - slot < seq_count - 1) & (slot - z < seq_count - 1)

        @pl.when(used)
        def _():
            for d in range(1, mp_count):
                to_peer(slot, d).wait_send()
            for reader in range(seq_count):
                @pl.when(is_sent(slot, reader)[0])
                def _():
                    to_reader(slot, reader).wait_send()


def tree_body(hidden, queries, w_kv, parents, lengths):
    rows, width = hidden.shape
    head_cols = w_kv.shape[1]
    count = lax.axis_size("seq")
    quarter = rows // count
    any_space = pl.BlockSpec(memory_space=pl.ANY)
    dma = pltpu.SemaphoreType.DMA
    return pl.pallas_call(
        tree_kernel,
        out_shape=jax.ShapeDtypeStruct(queries.shape, jnp.bfloat16),
        in_specs=[any_space] * 5,
        out_specs=pl.BlockSpec(memory_space=pltpu.VMEM),
        scratch_shapes=[
            pltpu.VMEM((count, rows, width), jnp.bfloat16),
            pltpu.VMEM(w_kv.shape, jnp.bfloat16),
            pltpu.VMEM(w_kv.shape, jnp.bfloat16),
            pltpu.VMEM(queries.shape, jnp.bfloat16),
            pltpu.VMEM((count + 1, rows, head_cols), jnp.float32),
            pltpu.VMEM((count + 1, count - 1, quarter, head_cols), jnp.float32),
            pltpu.VMEM((count + 1, quarter, head_cols), jnp.bfloat16),
            pltpu.VMEM((count, rows, head_cols), jnp.bfloat16),
            pltpu.VMEM((rows, count * rows), jnp.float32),
            pltpu.SMEM(parents.shape, jnp.int32),
            pltpu.SMEM(lengths.shape, jnp.int32),
            dma((5,)),
            dma((2, count, CHUNKS)),
            dma((count, CHUNKS)),
            dma((2, CHUNKS)),
            dma((2, CHUNKS)),
            dma((count + 1, count - 1)),
            dma((count + 1, count - 1)),
            dma((count + 1, count)),
            dma((count, count)),
        ],
        compiler_params=pltpu.CompilerParams(
            collective_id=0, has_side_effects=True, vmem_limit_bytes=56 * 1024 * 1024
        ),
    )(hidden, queries, w_kv, parents, lengths)


def solution(mesh):
    seq_count, mp_count = mesh.shape["seq"], mesh.shape["mp"]
    by_heads = seq_count == KVH and mp_count == KVH and mesh.shape["groups"] == 2
    return jax.shard_map(
        tree_body if by_heads else body,
        mesh=mesh,
        in_specs=(
            P(("groups", "seq"), "mp"),
            P(("groups", "seq"), "mp"),
            P("mp", "seq"),
            P("groups"),
            P("groups"),
        ),
        out_specs=P(("groups", "seq"), "mp"),
        check_vma=False,
    )
```

```python
import math

import jax
import jax.numpy as jnp
from jax import lax
from jax.experimental import pallas as pl
from jax.experimental.pallas import tpu as pltpu
from jax.sharding import PartitionSpec as P

HD = 128
KVH = 4
QH = 32
CHUNKS = 4
HALF = CHUNKS // 2
MESH = pl.DeviceIdType.MESH


def reach_table(parents, seg_count):
    seg_ids = jnp.arange(seg_count, dtype=jnp.int32)
    reach = (parents[:, None] == seg_ids[None, :]).astype(jnp.float32)
    for level in range(seg_count.bit_length()):
        reach = jnp.minimum(reach + jnp.dot(reach, reach, precision=lax.Precision.HIGHEST), 1.0)
    return reach


def body(hidden, queries, w_kv, parents, lengths):
    block_rows = hidden.shape[0]
    mp_count = lax.axis_size("mp")
    seq_count = lax.axis_size("seq")
    kv_heads = KVH // mp_count
    group = QH // KVH
    kv_terms = jnp.dot(
        hidden, lax.all_gather(w_kv, "seq", axis=1, tiled=True), preferred_element_type=jnp.float32
    )
    kv_sums = lax.psum_scatter(kv_terms, "mp", scatter_dimension=1, tiled=True)
    key_value = kv_sums.astype(jnp.bfloat16)
    my_index = lax.axis_index("seq")
    reach_row = reach_table(parents, seq_count)[my_index]
    query_heads = queries.reshape(block_rows, kv_heads, group, HD)
    q_offset = jnp.arange(block_rows, dtype=jnp.int32)
    score_scale = 1.0 / math.sqrt(HD)

    def update(carry, kv_block, allowed, own_block, k_offset):
        run_max, run_total, run_acc = carry
        split_kv = kv_block.reshape(kv_block.shape[0], kv_heads, 2, HD)
        scores = (
            jnp.einsum(
                "qhgd,khd->hgqk", query_heads, split_kv[:, :, 0], preferred_element_type=jnp.float32
            )
            * score_scale
        )
        key_mask = allowed[None, :] & (
            jnp.logical_not(own_block)[None, :] | (k_offset[None, :] <= q_offset[:, None])
        )
        scores = jnp.where(key_mask, scores, -1e30)
        new_max = jnp.maximum(run_max, scores.max(-1))
        factor = jnp.exp(run_max - new_max)
        weights = jnp.where(key_mask, jnp.exp(scores - new_max[..., None]), 0.0)
        run_total = run_total * factor + weights.sum(-1)
        run_acc = run_acc * factor[..., None] + jnp.einsum(
            "hgqk,khd->hgqd",
            weights.astype(jnp.bfloat16),
            split_kv[:, :, 1],
            preferred_element_type=jnp.float32,
        )
        return (new_max, run_total, run_acc)

    start_state = (
        jnp.full((kv_heads, group, block_rows), -1e30, jnp.float32),
        jnp.zeros((kv_heads, group, block_rows), jnp.float32),
        jnp.zeros((kv_heads, group, block_rows, HD), jnp.float32),
    )
    piece = lax.all_gather(key_value, "seq", axis=0, tiled=True)
    piece_rows = piece.shape[0]
    span = min(piece_rows, block_rows)

    def visit(position, state):
        kv_block = lax.dynamic_slice_in_dim(piece, position * span, span, 0)
        k_pos = position * span + jnp.arange(span, dtype=jnp.int32)
        k_block = k_pos // block_rows
        k_offset = k_pos % block_rows
        own_block = k_block == my_index
        allowed = (k_offset < lengths[k_block]) & (own_block | (reach_row[k_block] > 0.5))
        return lax.cond(
            jnp.any(allowed),
            lambda inner: update(inner, kv_block, allowed, own_block, k_offset),
            lambda inner: inner,
            state,
        )

    run_max, run_total, run_acc = lax.fori_loop(0, piece_rows // span, visit, start_state)
    summed = run_acc / run_total[..., None]
    summed = summed.transpose(2, 0, 1, 3).reshape(block_rows, kv_heads * group * HD)
    live_rows = q_offset < lengths[my_index]
    return jnp.where(live_rows[:, None], summed, 0.0).astype(jnp.bfloat16)


def tree_kernel(
    hidden_hbm, queries_hbm, w_hbm, parents_hbm, lengths_hbm, out_ref,
    hid, w, w_outer, q, acc, red, fin, kv, bias, parents_ref, lengths_ref,
    local_sem, hid_send, hid_recv, w_send, w_recv, red_send, red_recv, kv_send, kv_recv,
):
    seq_count, rows, width = hid.shape
    mp_count = seq_count
    quarter = rows // mp_count
    chunk = width // CHUNKS
    head_cols = w.shape[1]
    z = lax.axis_index("seq")
    m = lax.axis_index("mp")
    g = lax.axis_index("groups")
    is_end = (z == 0) | (z == seq_count - 1)
    is_inner = jnp.logical_not(is_end)
    inner = jnp.where(z == 0, 1, seq_count - 2)
    outer = jnp.where(z < seq_count // 2, 0, seq_count - 1)
    farthest = seq_count - 1 - outer
    extra = seq_count
    depth = w.shape[0] // 2
    piece = depth // CHUNKS

    hid_copy = pltpu.make_async_copy(hidden_hbm, hid.at[z], local_sem.at[0])
    w_copy = pltpu.make_async_copy(w_hbm, w, local_sem.at[1])
    q_copy = pltpu.make_async_copy(queries_hbm, q, local_sem.at[2])
    parents_copy = pltpu.make_async_copy(parents_hbm, parents_ref, local_sem.at[3])
    lengths_copy = pltpu.make_async_copy(lengths_hbm, lengths_ref, local_sem.at[4])
    hid_copy.start()
    parents_copy.start()
    lengths_copy.start()
    w_copy.start()
    q_copy.start()

    barrier = pltpu.get_barrier_semaphore()
    for dz in range(seq_count):
        for dm in range(mp_count):
            if dz or dm:
                pl.semaphore_signal(
                    barrier,
                    inc=1,
                    device_id={"seq": lax.rem(z + dz, seq_count), "mp": lax.rem(m + dm, mp_count)},
                    device_id_type=MESH,
                )

    pl.semaphore_signal(barrier, inc=1, device_id={"groups": 1 - g}, device_id_type=MESH)

    acc[...] = jnp.zeros_like(acc)
    for seg in range(seq_count):
        @pl.when(z < seg)
        def _():
            kv[seg] = jnp.zeros(kv.shape[1:], kv.dtype)

    parents_copy.wait()
    lengths_copy.wait()
    parent = [parents_ref[seg] for seg in range(seq_count)]
    def step_up(cur):
        up = jnp.int32(-1)
        for seg in range(seq_count):
            up = jnp.where(cur == seg, parent[seg], up)
        return up
    seen = [jnp.int32(0)] * seq_count
    cur = z
    for _ in range(seq_count - 1):
        cur = step_up(cur)
        seen = [jnp.where(cur == seg, 1, seen[seg]) for seg in range(seq_count)]
    q_pos = lax.broadcasted_iota(jnp.int32, (rows, rows), 0)
    k_pos = lax.broadcasted_iota(jnp.int32, (rows, rows), 1)
    my_length = jnp.int32(0)
    for seg in range(seq_count):
        own = z == seg
        my_length = jnp.where(own, lengths_ref[seg], my_length)
        limit = jnp.where((seen[seg] > 0) | own, lengths_ref[seg], 0)
        last = jnp.where(own, 0, rows)
        visible = (k_pos < limit) & (k_pos <= q_pos + last)
        bias[:, seg * rows:(seg + 1) * rows] = jnp.where(visible, 0.0, -1e30)

    pl.semaphore_wait(barrier, seq_count * mp_count)
    hid_copy.wait()

    def columns(c):
        return pl.ds(pl.multiple_of(c * chunk, chunk), chunk)

    def hop(way, seg, c):
        target = z + 1 if way == 0 else z - 1
        return pltpu.make_async_remote_copy(
            src_ref=hid.at[seg, :, columns(c)],
            dst_ref=hid.at[seg, :, columns(c)],
            send_sem=hid_send.at[way, seg, c],
            recv_sem=hid_recv.at[seg, c],
            device_id={"seq": target},
            device_id_type=MESH,
        )

    def add_chunk(seg, c):
        term = jnp.dot(
            hid[seg, :, columns(c)], w[columns(c), :], preferred_element_type=jnp.float32
        )
        acc[seg] += term

    def w_rows(half, c):
        return pl.ds(pl.multiple_of(half * depth + c * piece, piece), piece)

    def w_hop(c):
        return pltpu.make_async_remote_copy(
            src_ref=w.at[w_rows(g, c), :],
            dst_ref=w_outer.at[w_rows(g, c), :],
            send_sem=w_send.at[0, c],
            recv_sem=w_recv.at[0, c],
            device_id={"seq": inner},
            device_id_type=MESH,
        )

    def w_share(c):
        return pltpu.make_async_remote_copy(
            src_ref=w_outer.at[w_rows(g, c), :],
            dst_ref=w_outer.at[w_rows(g, c), :],
            send_sem=w_send.at[1, c],
            recv_sem=w_recv.at[1, c],
            device_id={"groups": 1 - g},
            device_id_type=MESH,
        )

    def add_half(half):
        part = pl.ds(pl.multiple_of(half * depth, depth), depth)
        acc[extra] += jnp.dot(
            hid[farthest, :, part], w_outer[part, :], preferred_element_type=jnp.float32
        )

    def to_peer(seg, d):
        peer = lax.rem(m + d, mp_count)
        return pltpu.make_async_remote_copy(
            src_ref=acc.at[seg, pl.ds(pl.multiple_of(peer * quarter, quarter), quarter), :],
            dst_ref=red.at[seg, d - 1],
            send_sem=red_send.at[seg, d - 1],
            recv_sem=red_recv.at[seg, d - 1],
            device_id={"mp": peer},
            device_id_type=MESH,
        )

    my_rows = pl.ds(pl.multiple_of(m * quarter, quarter), quarter)

    def to_reader(slot, reader):
        seg = jnp.where(slot == extra, farthest, slot)
        head = jnp.where(slot == extra, outer, z)
        return pltpu.make_async_remote_copy(
            src_ref=fin.at[slot],
            dst_ref=kv.at[seg, my_rows, :],
            send_sem=kv_send.at[slot, reader],
            recv_sem=kv_recv.at[seg, m],
            device_id={"seq": reader, "mp": head},
            device_id_type=MESH,
        )

    def send_terms(seg):
        for d in range(1, mp_count):
            to_peer(seg, d).start()

    def is_sent(slot, reader):
        seg = jnp.where(slot == extra, farthest, slot)
        head = jnp.where(slot == extra, outer, z)
        here = (z == reader) & (m == head)
        return (seg <= reader) & jnp.logical_not(here), (seg <= reader) & here

    def finish(slot):
        total = acc[slot, my_rows, :]
        for d in range(1, mp_count):
            to_peer(slot, d).wait_recv()
            total = total + red[slot, d - 1]
        fin[slot] = total.astype(fin.dtype)
        for reader in range(seq_count):
            away, here = is_sent(slot, reader)

            @pl.when(away)
            def _():
                to_reader(slot, reader).start()

            @pl.when(here)
            def _():
                kv[jnp.where(slot == extra, farthest, slot), my_rows, :] = fin[slot]

    def when_seg(seg, action):
        @pl.when((seg >= 0) & (seg < seq_count))
        def _():
            action(seg)

    for c in range(CHUNKS):
        @pl.when(z < seq_count - 1)
        def _():
            hop(0, z, c).start()

        @pl.when(z > 0)
        def _():
            hop(1, z, c).start()

    w_copy.wait()

    @pl.loop(0, CHUNKS)
    def _(c):
        add_chunk(z, c)

    send_terms(z)

    def pass_on(d, first):
        below, above = z - d, z + d
        forward = d < seq_count - 2

        @pl.loop(first, first + HALF)
        def _(c):
            @pl.when(below >= 0)
            def _():
                hop(0, below, c).wait_recv()
                if forward:
                    @pl.when(z < seq_count - 1)
                    def _():
                        hop(0, below, c).start()

            @pl.when(above < seq_count)
            def _():
                hop(1, above, c).wait_recv()
                if forward:
                    @pl.when(z > 0)
                    def _():
                        hop(1, above, c).start()

            @pl.when(below >= 0)
            def _():
                add_chunk(below, c)

            @pl.when(above < seq_count)
            def _():
                add_chunk(above, c)

            if d == seq_count - 2:
                @pl.when(is_inner)
                def _():
                    w_hop(c).wait_recv()
                    w_share(c).start()

    for d in range(1, seq_count - 1):
        pass_on(d, 0)
        if d == 1:
            finish(z)
        else:
            when_seg(z - d + 1, finish)
            when_seg(z + d - 1, finish)
        pass_on(d, HALF)
        if d == 1:
            @pl.when(is_end)
            def _():
                for c in range(CHUNKS):
                    @pl.when(z == 0)
                    def _():
                        hop(0, z, c).wait_send()

                    @pl.when(z > 0)
                    def _():
                        hop(1, z, c).wait_send()

                for c in range(CHUNKS):
                    w_hop(c).start()

        when_seg(z - d, send_terms)
        when_seg(z + d, send_terms)

    @pl.when(is_inner)
    def _():
        add_half(g)
        for c in range(CHUNKS):
            w_share(c).wait_recv()
        add_half(1 - g)
        send_terms(extra)

    when_seg(z - seq_count + 2, finish)
    when_seg(z + seq_count - 2, finish)

    @pl.when(is_inner)
    def _():
        finish(jnp.int32(extra))

    q_copy.wait()
    for seg in range(seq_count):
        for part in range(mp_count):
            source = jnp.where((m == 0) & (seg == seq_count - 1), 1, m)
            source = jnp.where((m == seq_count - 1) & (seg == 0), seq_count - 2, source)

            @pl.when((seg <= z) & ((z != source) | (m != part)))
            def _():
                pltpu.make_async_copy(
                    fin.at[seg], kv.at[seg, part * quarter:(part + 1) * quarter, :], kv_recv.at[seg, part]
                ).wait()

    keys = seq_count * rows
    scale = math.log2(math.e) / math.sqrt(HD)
    all_kv = kv[...].reshape(keys, head_cols)
    k_all = all_kv[:, :HD]
    v_all = all_kv[:, HD:]
    live = lax.broadcasted_iota(jnp.int32, (rows, HD), 0) < my_length
    for head in range(q.shape[1] // HD):
        cols = slice(head * HD, (head + 1) * HD)
        scores = lax.dot_general(
            q[:, cols], k_all, (((1,), (1,)), ((), ())), preferred_element_type=jnp.float32
        ) + bias[...]
        top = scores.max(-1, keepdims=True)
        weights = jnp.exp2((scores - top) * scale)
        total = weights.sum(-1, keepdims=True)
        summed = jnp.dot(
            weights.astype(jnp.bfloat16), v_all, preferred_element_type=jnp.float32
        ) / total
        out_ref[:, cols] = jnp.where(live, summed, 0.0).astype(out_ref.dtype)

    for c in range(CHUNKS):
        for seg in range(seq_count):
            @pl.when((seg <= z) & (z - seg < seq_count - 2) & (z < seq_count - 1) & (z > 0))
            def _():
                hop(0, seg, c).wait_send()

            @pl.when((seg >= z) & (seg - z < seq_count - 2) & (z < seq_count - 1) & (z > 0))
            def _():
                hop(1, seg, c).wait_send()

        @pl.when(is_end)
        def _():
            w_hop(c).wait_send()

        @pl.when(is_inner)
        def _():
            w_share(c).wait_send()

    for slot in range(seq_count + 1):
        used = is_inner if slot == extra else (z - slot < seq_count - 1) & (slot - z < seq_count - 1)

        @pl.when(used)
        def _():
            for d in range(1, mp_count):
                to_peer(slot, d).wait_send()
            for reader in range(seq_count):
                @pl.when(is_sent(slot, reader)[0])
                def _():
                    to_reader(slot, reader).wait_send()


def tree_body(hidden, queries, w_kv, parents, lengths):
    rows, width = hidden.shape
    head_cols = w_kv.shape[1]
    count = lax.axis_size("seq")
    quarter = rows // count
    any_space = pl.BlockSpec(memory_space=pl.ANY)
    dma = pltpu.SemaphoreType.DMA
    return pl.pallas_call(
        tree_kernel,
        out_shape=jax.ShapeDtypeStruct(queries.shape, jnp.bfloat16),
        in_specs=[any_space] * 5,
        out_specs=pl.BlockSpec(memory_space=pltpu.VMEM),
        scratch_shapes=[
            pltpu.VMEM((count, rows, width), jnp.bfloat16),
            pltpu.VMEM(w_kv.shape, jnp.bfloat16),
            pltpu.VMEM(w_kv.shape, jnp.bfloat16),
            pltpu.VMEM(queries.shape, jnp.bfloat16),
            pltpu.VMEM((count + 1, rows, head_cols), jnp.float32),
            pltpu.VMEM((count + 1, count - 1, quarter, head_cols), jnp.float32),
            pltpu.VMEM((count + 1, quarter, head_cols), jnp.bfloat16),
            pltpu.VMEM((count, rows, head_cols), jnp.bfloat16),
            pltpu.VMEM((rows, count * rows), jnp.float32),
            pltpu.SMEM(parents.shape, jnp.int32),
            pltpu.SMEM(lengths.shape, jnp.int32),
            dma((5,)),
            dma((2, count, CHUNKS)),
            dma((count, CHUNKS)),
            dma((2, CHUNKS)),
            dma((2, CHUNKS)),
            dma((count + 1, count - 1)),
            dma((count + 1, count - 1)),
            dma((count + 1, count)),
            dma((count, count)),
        ],
        compiler_params=pltpu.CompilerParams(
            collective_id=0, has_side_effects=True, vmem_limit_bytes=56 * 1024 * 1024
        ),
    )(hidden, queries, w_kv, parents, lengths)


def solution(mesh):
    seq_count, mp_count = mesh.shape["seq"], mesh.shape["mp"]
    by_heads = seq_count == KVH and mp_count == KVH and mesh.shape["groups"] == 2
    return jax.shard_map(
        tree_body if by_heads else body,
        mesh=mesh,
        in_specs=(
            P(("groups", "seq"), "mp"),
            P(("groups", "seq"), "mp"),
            P("mp", "seq"),
            P("groups"),
            P("groups"),
        ),
        out_specs=P(("groups", "seq"), "mp"),
        check_vma=False,
    )
```
